128 devices in a mesh: gx: 16 (over z, y), gy: 8 (over x, core).
Axes of the slice: x: 4, y: 4, z: 4, core: 2. Of those that a mesh axis runs over, the one named last changes fastest.
Arguments:
- template: bfloat16 [512, 256, 256], P('gx', 'gy'), may hold values from -6 to 6
- target_image: bfloat16 [512, 256, 256], P('gx', 'gy'), may hold values from -6 to 6
- velocity: float32 [3, 512, 256, 256], P(None, 'gx', 'gy'), may hold values from -6 to 6
- operators: bfloat16 [64, 3, 32, 32], replicated, may hold values from -1 to 1
- route: int32 [2, 16, 8, 8, 1], P(None, 'gx', 'gy'), may hold values from 0 to 15; in each aligned block of 8 rows (0 to 7, 8 to 15, ..., all dimensions but the last counted through in order) at most 2 rows name the same one
- target_brick: int32 [2, 16, 8, 8], P(None, 'gx', 'gy'), may hold values from 0 to 7
- operator_index: int32 [2, 16, 8, 8], P(None, 'gx', 'gy'), may hold values from 0 to 63
Outputs:
- velocity_grad: float32 [3, 512, 256, 256], P(None, 'gx', 'gy')
- template_grad: bfloat16 [512, 256, 256], P('gx', 'gy')
The draws below stay inside these ranges and needn't reach their ends.
Inputs may be any that keep to these rules, and one draw needn't show every extreme that they name: `route`: in every step, no device sends more than 2 of its bricks to one destination device, and some device sends exactly 2 to one; the destination keeps the second index.
All inputs are finite; a program needn't handle non-finite values.
Results may differ from the reference program's by a relative error of at most 0.0085.
Values may be sent and summed in bfloat16 or wider, within the bound.
A program may use at most 128 MiB of HBM per device.

```python
import math
import jax
import jax.numpy as jnp
import numpy as np
from jax import lax

BE = 32
ZB = 8
STEPS = 2
NW = 64
CAP = 2
ROWS_X = 16
ROWS_Y = 8
NX = 512
NY = 256
NZ = 256


def touch_ends(result, own_key, smallest, high):
    place = [jax.random.randint(jax.random.fold_in(own_key, axis), (), 0, length) for axis, length in enumerate(result.shape)]
    widest = result.shape.index(max(result.shape))
    neighbour = place[:widest] + [(place[widest] + 1) % result.shape[widest]] + place[widest + 1:]
    return result.at[tuple(place)].set(smallest).at[tuple(neighbour)].set(high)


def level_of(own_key, extent, cuts, smallest, top_value):
    gain = 1.0
    for position, blocks in cuts:
        draws = jax.random.uniform(jax.random.fold_in(jax.random.fold_in(own_key, 6), position), (blocks,), jnp.float32, smallest / len(cuts), top_value / len(cuts))
        gain = gain * jnp.repeat(jnp.exp(draws), extent[position] // blocks).reshape((-1,) + (1,) * (len(extent) - 1 - position))
    return gain


def deal_out(key, own, number, rows, amount, top, limit, lean):
    order = jax.random.permutation(key, amount)
    packed, usual = load_shares(amount, rows * top, limit, lean, True), load_shares(amount, rows * top, limit, lean, False)
    places = jnp.arange(amount)

    def named(lengths, turn):
        used = int((lengths > 0).sum())
        fixed = max(1, used // 4)
        moved = fixed + (places - fixed + turn * (used - fixed)) % max(1, amount - fixed)
        return jnp.zeros((amount,), jnp.int32).at[order[jnp.where(places < fixed, places, moved)]].set(jnp.asarray(lengths, jnp.int32))

    lengths = jnp.where(number % 4 == 0, named(packed, number // 4), named(usual, number - number // 4 - 1))
    mixed = jax.random.permutation(jax.random.fold_in(own, 3), amount)
    giver, sink = mixed[0:amount // 2 * 2:2], mixed[1:amount // 2 * 2:2]
    slack = jnp.minimum(lengths[giver] - 1, limit - lengths[sink]) // 2
    slack = jnp.where((giver == order[0]) | (sink == order[0]) | (lengths[sink] == 0), 0, jnp.maximum(slack, 0))
    moved = jax.random.randint(jax.random.fold_in(own, 4), (amount // 2,), 0, 1 << 20) % (slack + 1)
    lengths = lengths.at[giver].add(-moved).at[sink].add(moved)
    members = jnp.searchsorted(jnp.cumsum(lengths), jnp.arange(rows * top), side="right").astype(jnp.int32)
    listing = members.reshape(top, rows).T
    listing = listing[jax.random.permutation(jax.random.fold_in(own, 1), rows)]
    turn = jax.random.randint(jax.random.fold_in(own, 2), (rows, 1), 0, top)
    return jnp.take_along_axis(listing, (jnp.arange(top)[None, :] + turn) % top, axis=1)


def load_shares(number_of, total, limit, skew, full):
    loads = [(1 << 20) // math.isqrt(standing ** skew) + 1 for standing in range(1, number_of + 1)]
    largest = limit if full else min(limit, max(-(-total // number_of), total * loads[0] // sum(loads)))
    least = 1 if total - largest >= number_of - 1 else 0
    given, rest = [largest] + [least] * (number_of - 1), total - largest - least * (number_of - 1)
    while rest > 0:
        movable = [i for i in range(1, number_of) if given[i] < largest] or [i for i in range(1, number_of) if given[i] < limit]
        mass, budget = sum([loads[i] for i in movable]), rest
        for i in movable:
            more = min(limit - given[i], max(1, budget * loads[i] // mass), rest)
            given[i] = given[i] + more
            rest = rest - more
    return np.array(given)


def normal_values(stream_key, extent, spread, most, cuts=(), held_as=jnp.bfloat16):
    level = level_of(stream_key, extent, cuts, -0.22, 0.18) if cuts else 1.0
    result = jax.random.normal(stream_key, extent, jnp.float32) * spread * level
    return jnp.minimum(jnp.maximum(result, -most), most).astype(held_as)


def setup_inputs(seed: int = 0) -> dict:
    splits = jax.random.split(jax.random.key(seed), 8)
    template = normal_values(splits[0], (NX, NY, NZ), 1.0, 6.0, ((0, 16), (1, 8)))
    target_image = normal_values(splits[1], (NX, NY, NZ), 1.0, 6.0, ((0, 16), (1, 8)))
    velocity = normal_values(splits[2], (3, NX, NY, NZ), 1.0, 6.0, ((1, 16), (2, 8)), jnp.float32)
    operators = normal_values(splits[3], (NW, 3, BE, BE), BE ** -0.5, 1.0)
    route_keys = jax.random.split(jax.random.fold_in(splits[4], 1), STEPS * ROWS_X * ROWS_Y * ZB // ZB)
    route_turns = jax.random.permutation(jax.random.fold_in(splits[4], 3), STEPS * ROWS_X * ROWS_Y * ZB // ZB)
    route = jax.vmap(lambda own, number: deal_out(jax.random.fold_in(splits[4], 2), own, number, ZB, ROWS_X, 1, CAP, 2))(route_keys, route_turns).reshape((STEPS, ROWS_X, ROWS_Y, ZB, 1))
    target_brick = touch_ends(jax.random.randint(splits[5], (STEPS, ROWS_X, ROWS_Y, ZB), 0, ZB), jax.random.fold_in(splits[5], 1), 0, ZB - 1).astype(jnp.int32)
    operator_index = touch_ends(jax.random.randint(splits[6], (STEPS, ROWS_X, ROWS_Y, ZB), 0, NW), jax.random.fold_in(splits[6], 1), 0, NW - 1).astype(jnp.int32)
    return {"template": template, "target_image": target_image, "velocity": velocity, "operators": operators, "route": route, "target_brick": target_brick, "operator_index": operator_index}


HIGHEST_PRECISION = lax.Precision.HIGHEST


def to_bricks(field_in):
    shaped = field_in.reshape(ROWS_X, BE, ROWS_Y, BE, ZB, BE)
    return shaped.transpose(0, 2, 4, 1, 3, 5)


def from_bricks(bricks):
    return bricks.transpose(0, 3, 1, 4, 2, 5).reshape(ROWS_X * BE, ROWS_Y * BE, ZB * BE)


def apply_operator(matrices, bricks, flipped):
    matrices = matrices.astype(jnp.float32)
    values_f = bricks.astype(jnp.float32)
    if flipped:
        forms_list = ["...ax,...abc->...xbc", "...by,...xbc->...xyc", "...cz,...xyc->...xyz"]
    else:
        forms_list = ["...xa,...abc->...xbc", "...yb,...xbc->...xyc", "...zc,...xyc->...xyz"]
    for axis_id in range(3):
        values_f = jnp.einsum(forms_list[axis_id], matrices[..., axis_id, :, :], values_f, precision=HIGHEST_PRECISION)
    return values_f


def sixth_order(padded, axis_id):
    array_rank = padded.ndim

    def shifted(offset):
        slicer = []
        for dimension in range(array_rank):
            if dimension < array_rank - 3:
                slicer.append(slice(None))
            elif dimension == array_rank - 3 + axis_id:
                slicer.append(slice(3 + offset, padded.shape[dimension] - 3 + offset))
            else:
                slicer.append(slice(3, padded.shape[dimension] - 3))
        return padded[tuple(slicer)]

    return 0.75 * (shifted(1) - shifted(-1)) - 0.15 * (shifted(2) - shifted(-2)) + (shifted(3) - shifted(-3)) / 60.0


def pad_grid(field_in):
    widths = [(0, 0)] * (field_in.ndim - 3) + [(3, 3)] * 3
    return jnp.pad(field_in, widths)


def reference(template, target_image, velocity, operators, route, target_brick, operator_index):
    column = jnp.arange(ROWS_Y, dtype=jnp.int32)[None, :, None]
    states = [template]
    for section_id in range(STEPS):
        bricks = to_bricks(states[-1])
        matrices = operators[operator_index[section_id]]
        moved_bricks = apply_operator(matrices, bricks, False).astype(jnp.bfloat16)
        totals = jnp.zeros(bricks.shape, jnp.float32)
        totals = totals.at[route[section_id, :, :, :, 0], column, target_brick[section_id]].add(moved_bricks.astype(jnp.float32))
        states.append(from_bricks(totals.astype(jnp.bfloat16)))
    adjoint = (states[-1].astype(jnp.float32) - target_image.astype(jnp.float32)).astype(jnp.bfloat16)
    accumulated = jnp.zeros((3,) + template.shape, jnp.float32)
    for section_id in reversed(range(STEPS)):
        padded = pad_grid(states[section_id].astype(jnp.float32))
        weight = adjoint.astype(jnp.float32)
        accumulated = accumulated + jnp.stack([weight * sixth_order(padded, axis_id) for axis_id in range(3)])
        pulled = to_bricks(adjoint)[route[section_id, :, :, :, 0], column, target_brick[section_id]]
        matrices = operators[operator_index[section_id]]
        adjoint = from_bricks(apply_operator(matrices, pulled, True).astype(jnp.bfloat16))
    velocity_pad = pad_grid(velocity)
    divergence = sixth_order(velocity_pad[0], 0) + sixth_order(velocity_pad[1], 1) + sixth_order(velocity_pad[2], 2)
    divergence_pad = pad_grid(divergence)
    regular = jnp.stack([sixth_order(divergence_pad, axis_id) for axis_id in range(3)])
    velocity_grad = accumulated / STEPS - 0.25 * regular
    return velocity_grad, adjoint
```

```python
import jax
import jax.numpy as jnp
from jax import lax
from jax.experimental import pallas as pl
from jax.experimental.pallas import tpu as pltpu
from jax.sharding import PartitionSpec as P

MESH = pl.DeviceIdType.MESH
F32 = jnp.float32
BF16 = jnp.bfloat16
E = 32
CH = 256
HF = 128


def mm(a, b):
    return jnp.dot(a, b, preferred_element_type=F32)


def mmt(a, b):
    return lax.dot_general(a, b, (((1,), (1,)), ((), ())), preferred_element_type=F32)


def iota(shape, dim):
    return lax.broadcasted_iota(jnp.int32, shape, dim)


def kernel(
    idx_ref, tmpl, targ_hbm, vel_hbm, ops_ref, vg_hbm, tg_ref,
    f1, mv, gg, r3, r12, ps, pf, sel, lhs, wc, ost, mask, tile, dz, targ,
    qs0, qs1, qd, qv0, qv1, v2, out, s1f, l1f, hx, hxs, hy, meta, mz, my,
    xs, xr, hs, hr, ms, mr, ls,
):
    gx = lax.axis_index("gx")
    gy = lax.axis_index("gy")
    z = gx // 4
    y = gx % 4

    def at(dz_, dy_):
        return ((z + dz_) % 4) * 4 + (y + dy_) % 4

    xlo, xhi = (gx + 15) % 16, (gx + 1) % 16
    ylo, yhi = (gy + 7) % 8, (gy + 1) % 8
    peers = [at(1, 0), at(2, 0), at(3, 0), at(0, 1), at(0, 2), at(0, 3)]

    loads = [
        pltpu.make_async_copy(vel_hbm.at[0], qv0.at[pl.ds(3, E)], ls.at[0]),
        pltpu.make_async_copy(vel_hbm.at[1], qv1.at[:, pl.ds(8, E), :], ls.at[1]),
        pltpu.make_async_copy(vel_hbm.at[2], v2, ls.at[2]),
        pltpu.make_async_copy(targ_hbm, targ, ls.at[3]),
    ]
    for c in loads:
        c.start()

    barrier = pltpu.get_barrier_semaphore()
    for p in peers + [xlo, xhi]:
        pl.semaphore_signal(barrier, inc=1, device_id={"gx": p}, device_id_type=MESH)
    for p in (ylo, yhi):
        pl.semaphore_signal(barrier, inc=1, device_id={"gy": p}, device_id_type=MESH)

    lane_b = iota((8, 256), 1) // E
    row_t = iota((8, 256), 0)
    m = jnp.zeros((8, 256), jnp.int32)
    for t in range(2):
        for b in range(8):
            m = jnp.where((row_t == t) & (lane_b == b), idx_ref[1, t * 8 + b], m)
    meta[...] = m

    mask[...] = jnp.where(iota((256, 256), 0) // E == iota((256, 256), 1) // E, 1.0, 0.0).astype(BF16)
    tile[...] = jnp.where(iota((E, 256), 0) == iota((E, 256), 1) % E, 1.0, 0.0).astype(BF16)

    def build(t):
        for b in range(8):
            w = ops_ref[idx_ref[0, t * 8 + b]]
            for k in range(3):
                ost[t, k, b * E:(b + 1) * E, :] = w[k * E:(k + 1) * E, :]
        for k in range(2):
            for j in range(2):
                part = ost[t, k, j * 128:(j + 1) * 128, :]
                spread = mm(part, tile[:, 0:128]) * mask[0:128, 0:128].astype(F32)
                lhs[t, k, 0, j] = (spread[0:32] + spread[32:64] + spread[64:96] + spread[96:128]).astype(BF16)
                lhs[t, k, 1, j] = mmt(tile[:, 0:E], part).astype(BF16)
        wc[t] = (mm(ost[t, 2], tile[...]) * mask[...].astype(F32)).astype(BF16)

    build(0)

    pl.semaphore_wait(barrier, 10)

    sends = []

    def send(src, dst, ssem, rsem, dev):
        c = pltpu.make_async_remote_copy(
            src_ref=src, dst_ref=dst, send_sem=ssem, recv_sem=rsem, device_id=dev, device_id_type=MESH
        )
        return c

    metas = []
    for i, (buf, d) in enumerate([(mz, 1), (mz, 2), (mz, 3), (my, 1), (my, 2), (my, 3)]):
        dev = at(d, 0) if i < 3 else at(0, d)
        metas.append(send(meta, buf.at[3 - d], ms.at[i], mr.at[(0 if i < 3 else 3) + 3 - d], {"gx": dev}))
    for c in metas:
        c.start()

    def halo_x(f, low, high):
        return [
            send(low, hx.at[f, 1], hs.at[f, 0], hr.at[f, 0], {"gx": xlo}),
            send(high, hx.at[f, 0], hs.at[f, 1], hr.at[f, 1], {"gx": xhi}),
        ]

    def halo_y(f, low, high):
        return [
            send(low, hy.at[f, 1], hs.at[f, 2], hr.at[f, 2], {"gy": ylo}),
            send(high, hy.at[f, 0], hs.at[f, 3], hr.at[f, 3], {"gy": yhi}),
        ]

    def contract(t, k, tr, load, store):
        for i in range(8):
            for j in range(2):
                part = load(i, j)
                big = jnp.concatenate([part] * 4, axis=0) * mask[0:128, 0:128]
                store(i, j, mm(lhs[t, k, tr, j], big))

    def first(t, k, tr, row0, value):
        def load(i, j):
            return value[i * E:(i + 1) * E, j * 128:(j + 1) * 128]

        def store(i, j, res):
            f1[j, pl.ds(row0 + i * E, E), :] = res

        contract(t, k, tr, load, store)

    def second(t, k, tr, row0):
        got = [[None, None] for _ in range(8)]

        def load(i, j):
            return f1[j, pl.ds(row0 // E + i, E, stride=E), :].astype(BF16)

        def store(i, j, res):
            got[i][j] = res

        contract(t, k, tr, load, store)
        rows = [jnp.concatenate(g, axis=1) for g in got]
        return jnp.concatenate(rows, axis=0)

    def row_of(u):
        return pl.multiple_of((u % 2) * 512 + (u // 2) * CH, CH)

    def axes(p, u):
        a = (1 - u % 2) if p < 2 else u % 2
        gather = (at(a, 1 - a), at(3 * a, 3 * (1 - a)))
        scatter = (at(1 - a, a), at(3 * (1 - a), 3 * a))
        return gather, scatter

    def xcopy(p, u, n):
        (gp, gm), (sp, sm) = axes(p, u)
        own = mv.at[p, pl.ds(row_of(u), CH)]
        top, low = pl.ds(0, HF), pl.ds(HF, HF)
        src, dst, dev = [
            (own, gg.at[p, u, 0], gp),
            (own, gg.at[p, u, 1], gm),
            (gg.at[p, u, 0, top], gg.at[p, u, 2, top], gp),
            (gg.at[p, u, 1, low], gg.at[p, u, 2, low], gm),
            (ps.at[p, u, 0, top], r3.at[p, u, top], sp),
            (ps.at[p, u, 0, low], r3.at[p, u, low], sm),
            (ps.at[p, u, 1], r12.at[p, u, 0], sp),
            (ps.at[p, u, 2], r12.at[p, u, 1], sm),
        ][n]
        return send(src, dst, xs.at[p, u, n], xr.at[p, u, n], {"gx": dev})

    def units(body):
        def step(u, carry):
            body(u)
            return carry
        lax.fori_loop(0, 4, step, 0)

    def gather_start(p, u):
        xcopy(p, u, 0).start()
        xcopy(p, u, 1).start()

    def gather_on(p):
        def body(u):
            xcopy(p, u, 0).wait_recv()
            xcopy(p, u, 2).start()
            xcopy(p, u, 1).wait_recv()
            xcopy(p, u, 3).start()
        units(body)

    def pick(p, t):
        def body(u):
            xcopy(p, u, 2).wait_recv()
            xcopy(p, u, 3).wait_recv()
            h = u % 2
            blocks = [mv[p, pl.ds(row_of(u), CH), :], gg[p, u, 1], gg[p, u, 2], gg[p, u, 0]]

            def part(o):
                total = None
                for s in range(4):
                    v = mmt(blocks[s], sel[t, h, o, s]) if p < 2 else mm(blocks[s], sel[t, h, s, o])
                    total = v if total is None else total + v
                return total

            ps[p, u, 0] = part(2).astype(BF16)
            xcopy(p, u, 4).start()
            xcopy(p, u, 5).start()
            pf[u, 0] = part(1)
            pf[u, 1] = part(3)
            pf[u, 2] = part(0)
        units(body)

    def scatter_on(p):
        def body(u):
            xcopy(p, u, 4).wait_recv()
            ps[p, u, 1, 0:HF, :] = (pf[u, 0, 0:HF, :] + r3[p, u, 0:HF, :].astype(F32)).astype(BF16)
            ps[p, u, 1, HF:CH, :] = pf[u, 0, HF:CH, :].astype(BF16)
            xcopy(p, u, 6).start()
            xcopy(p, u, 5).wait_recv()
            ps[p, u, 2, 0:HF, :] = pf[u, 1, 0:HF, :].astype(BF16)
            ps[p, u, 2, HF:CH, :] = (pf[u, 1, HF:CH, :] + r3[p, u, HF:CH, :].astype(F32)).astype(BF16)
            xcopy(p, u, 7).start()
        units(body)

    def arrived(p, u):
        xcopy(p, u, 6).wait_recv()
        xcopy(p, u, 7).wait_recv()
        return pf[u, 2] + r12[p, u, 0].astype(F32) + r12[p, u, 1].astype(F32)

    def build_sel(t):
        row = iota((256, 256), 0)
        same = row % E == iota((256, 256), 1) % E
        row_e = row // E
        for h in range(2):
            for s in range(4):
                raw = (meta if s == 0 else (mz, my)[h].at[s - 1])[t:t + 1, :]
                rz, ry, e = raw >> 5, (raw >> 3) & 3, raw & 7
                if h == 0:
                    key = jnp.where(rz == z, (((ry - y) & 3) << 3) | e, -1)
                else:
                    key = jnp.where(ry == y, (((rz - z) & 3) << 3) | e, -1)
                key = jnp.broadcast_to(key, (256, 256))
                for o in range(4):
                    sel[t, h, o, s] = jnp.where(same & (row_e + 8 * o == key), 1.0, 0.0).astype(BF16)

    xl = jnp.where(gx > 0, 1.0, 0.0).astype(F32)
    xh = jnp.where(gx < 15, 1.0, 0.0).astype(F32)
    yl = jnp.where(gy > 0, 1.0, 0.0).astype(F32)
    yh = jnp.where(gy < 7, 1.0, 0.0).astype(F32)

    def rim_x(f, q, off):
        for i in range(3):
            q[i, off:off + E, :] = hx[f, 0, i * E:(i + 1) * E, :].astype(F32) * xl
            q[E + 3 + i, off:off + E, :] = hx[f, 1, i * E:(i + 1) * E, :].astype(F32) * xh

    def rim_y(f, q, off):
        def step(i, c):
            q[off + i, 0:8, :] = hy[f, 0, i] * yl
            q[off + i, 40:48, :] = hy[f, 1, i] * yh
            return c
        lax.fori_loop(0, E, step, 0)

    def combine(p1, m1, p2, m2, p3, m3):
        return 0.75 * (p1 - m1) - 0.15 * (p2 - m2) + (p3 - m3) * (1.0 / 60.0)

    def d_x(q, i, off):
        at_ = [q[i + n, off:off + E, :] for n in range(7)]
        return combine(at_[4], at_[2], at_[5], at_[1], at_[6], at_[0])

    def d_y(q, i):
        at_ = [q[i, 5 + n:5 + n + E, :] for n in range(7)]
        return combine(at_[4], at_[2], at_[5], at_[1], at_[6], at_[0])

    diff = iota((256, 256), 0) - iota((256, 256), 1)
    size = jnp.abs(diff)
    coef = jnp.where(size == 1, 0.75, 0.0) + jnp.where(size == 2, -0.15, 0.0) + jnp.where(size == 3, 1.0 / 60.0, 0.0)
    coef = jnp.where(diff < 0, -coef, coef).astype(F32)
    dz_hi = coef.astype(BF16)
    dz[0] = dz_hi
    dz[1] = (coef - dz_hi.astype(F32)).astype(BF16)

    def d_z(value, exact):
        hi = value.astype(BF16)
        total = mm(hi, dz[0]) + mm(hi, dz[1])
        if not exact:
            total = total + mm((value - hi.astype(F32)).astype(BF16), dz[0])
        return total

    def planes(lo, hi, body):
        def step(i, c):
            body(i)
            return c
        lax.fori_loop(lo, hi, step, 0)

    def gradient(q, weight, lo, hi, exact):
        def group(g):
            i0 = g * 8
            dzv = d_z(q[pl.ds(3 + i0, 8), 8:8 + E, :].reshape(8 * E, 256), exact)
            for n in range(8):
                i = i0 + n
                w = weight(i)
                part = dzv[n * E:(n + 1) * E]
                if w is None:
                    out[0, i] = -0.25 * d_x(q, i + 0, 8)
                    out[1, i] = -0.25 * d_y(q, i + 3)
                    out[2, i] = -0.25 * part
                else:
                    out[0, i] = out[0, i] + w * d_x(q, i, 8)
                    out[1, i] = out[1, i] + w * d_y(q, i + 3)
                    out[2, i] = out[2, i] + w * part
        planes(lo, hi, group)

    sends += halo_x(0, tmpl.at[pl.ds(0, 96)], tmpl.at[pl.ds(928, 96)])
    for c in sends:
        c.start()

    def chunk0(u):
        r = pl.multiple_of(u * CH, CH)
        first(0, 1, 0, r, tmpl[pl.ds(r, CH), :])
    units(chunk0)

    def forward_start(p, t, k):
        def body(u):
            r = row_of(u)
            mv[p, pl.ds(r, CH), :] = mmt(second(t, k, 0, r).astype(BF16), wc[t]).astype(BF16)
            gather_start(p, u)
        units(body)

    forward_start(0, 0, 0)

    def fill0(i):
        qs0[3 + i, 8:8 + E, :] = tmpl[pl.ds(pl.multiple_of(i * E, E), E), :].astype(F32)
    planes(0, E, fill0)
    for c in loads:
        c.wait()
    for i in range(3):
        hxs[0, 0, i * E:(i + 1) * E, :] = qv0[3 + i].astype(BF16)
        hxs[0, 1, i * E:(i + 1) * E, :] = qv0[E + i].astype(BF16)
    more = halo_y(0, qs0.at[pl.ds(3, E), pl.ds(8, 8), :], qs0.at[pl.ds(3, E), pl.ds(32, 8), :])
    more += halo_x(1, hxs.at[0, 0], hxs.at[0, 1])
    more += halo_y(1, qv1.at[:, pl.ds(8, 8), :], qv1.at[:, pl.ds(32, 8), :])
    for c in more:
        c.start()
    sends += more
    gather_on(0)
    for c in metas:
        c.wait_recv()
    build_sel(0)
    pick(0, 0)

    for c in more[2:6]:
        c.wait_recv()
    rim_x(1, qv0, 0)
    rim_y(1, qv1, 0)

    def div_group(g):
        i0 = g * 8
        dzv = d_z(v2[pl.ds(i0, 8)].reshape(8 * E, 256), False)
        for n in range(8):
            i = i0 + n
            qd[3 + i, 8:8 + E, :] = d_x(qv0, i, 0) + d_y(qv1, i) + dzv[n * E:(n + 1) * E]
    planes(0, 4, div_group)
    for i in range(3):
        hxs[1, 0, i * E:(i + 1) * E, :] = qd[3 + i, 8:8 + E, :].astype(BF16)
        hxs[1, 1, i * E:(i + 1) * E, :] = qd[E + i, 8:8 + E, :].astype(BF16)
    divs = halo_x(2, hxs.at[1, 0], hxs.at[1, 1])
    divs += halo_y(2, qd.at[pl.ds(3, E), pl.ds(8, 8), :], qd.at[pl.ds(3, E), pl.ds(32, 8), :])
    for c in divs:
        c.start()
    sends += divs
    scatter_on(0)
    build(1)

    def end0(u):
        r = row_of(u)
        s1 = arrived(0, u).astype(BF16)
        wide = s1.astype(F32)
        s1f[0, pl.ds(r, CH), :] = wide[:, 0:128]
        s1f[1, pl.ds(r, CH), :] = wide[:, 128:256]
        first(1, 0, 0, r, s1)
    units(end0)

    forward_start(1, 1, 1)

    def fill1(i):
        qs1[3 + i, 8:8 + E, 0:128] = s1f[0, pl.ds(i, E, stride=E), :]
        qs1[3 + i, 8:8 + E, 128:256] = s1f[1, pl.ds(i, E, stride=E), :]
    planes(0, E, fill1)
    for i in range(3):
        hxs[2, 0, i * E:(i + 1) * E, :] = qs1[3 + i, 8:8 + E, :].astype(BF16)
        hxs[2, 1, i * E:(i + 1) * E, :] = qs1[E + i, 8:8 + E, :].astype(BF16)
    ones = halo_x(3, hxs.at[2, 0], hxs.at[2, 1])
    ones += halo_y(3, qs1.at[pl.ds(3, E), pl.ds(8, 8), :], qs1.at[pl.ds(3, E), pl.ds(32, 8), :])
    for c in ones:
        c.start()
    sends += ones
    gather_on(1)
    build_sel(1)
    pick(1, 1)
    for c in divs:
        c.wait_recv()
    rim_x(2, qd, 8)
    rim_y(2, qd, 3)
    gradient(qd, lambda i: None, 0, 4, False)
    scatter_on(1)

    def end1(u):
        r = row_of(u)
        s2 = arrived(1, u).astype(BF16).astype(F32)
        mv[2, pl.ds(r, CH), :] = (s2 - targ[pl.ds(r, CH), :].astype(F32)).astype(BF16)
        gather_start(2, u)
    units(end1)

    for c in ones:
        c.wait_recv()
    rim_x(3, qs1, 8)
    rim_y(3, qs1, 3)

    def weight1(i):
        return 0.5 * mv[2, pl.ds(pl.multiple_of(i * E, E), E), :].astype(F32)
    gather_on(2)
    gradient(qs1, weight1, 0, 2, True)
    pick(2, 1)
    gradient(qs1, weight1, 2, 4, True)
    scatter_on(2)

    def end2(u):
        r = row_of(u)
        back = arrived(2, u).astype(BF16)
        first(1, 1, 1, r, mm(back, wc[1]).astype(BF16))
    units(end2)

    def adjoint_start(u):
        r = row_of(u)
        l1 = second(1, 0, 1, r).astype(BF16)
        mv[3, pl.ds(r, CH), :] = l1
        gather_start(3, u)
        wide = l1.astype(F32) * 0.5
        l1f[0, pl.ds(r, CH), :] = wide[:, 0:128]
        l1f[1, pl.ds(r, CH), :] = wide[:, 128:256]
    units(adjoint_start)

    for c in sends[0:4]:
        c.wait_recv()
    rim_x(0, qs0, 8)
    rim_y(0, qs0, 3)

    def weight0(i):
        return jnp.concatenate(
            [l1f[0, pl.ds(i, E, stride=E), :], l1f[1, pl.ds(i, E, stride=E), :]], axis=1
        )
    gather_on(3)
    gradient(qs0, weight0, 0, 2, True)
    pick(3, 0)
    gradient(qs0, weight0, 2, 4, True)
    save = pltpu.make_async_copy(out, vg_hbm, ls.at[4])
    save.start()
    scatter_on(3)

    def end3(u):
        r = row_of(u)
        back = arrived(3, u).astype(BF16)
        first(0, 0, 1, r, mm(back, wc[0]).astype(BF16))
    units(end3)

    def finish(u):
        r = row_of(u)
        tg_ref[pl.ds(r, CH), :] = second(0, 1, 1, r).astype(BF16)
    units(finish)

    for c in metas + sends:
        c.wait_send()
    for p in range(4):
        def drain(u, p=p):
            for n in range(8):
                xcopy(p, u, n).wait_send()
        units(drain)
    save.wait()


def shards(template, target_image, velocity, operators, route, target_brick, operator_index):
    index = jnp.stack(
        [operator_index.reshape(16), route.reshape(16) * 8 + target_brick.reshape(16)]
    )
    vmem = pl.BlockSpec(memory_space=pltpu.VMEM)
    hbm = pl.BlockSpec(memory_space=pl.ANY)
    field = (E + 6, E + 16, 256)
    dma = pltpu.SemaphoreType.DMA
    vg, tg = pl.pallas_call(
        kernel,
        out_shape=(
            jax.ShapeDtypeStruct((3, E, E, 256), F32),
            jax.ShapeDtypeStruct((1024, 256), BF16),
        ),
        in_specs=[pl.BlockSpec(memory_space=pltpu.SMEM), vmem, hbm, hbm, vmem],
        out_specs=(hbm, vmem),
        scratch_shapes=[
            pltpu.VMEM((2, 1024, 128), F32),
            pltpu.VMEM((4, 1024, 256), BF16),
            pltpu.VMEM((4, 4, 3, CH, 256), BF16),
            pltpu.VMEM((4, 4, CH, 256), BF16),
            pltpu.VMEM((4, 4, 2, CH, 256), BF16),
            pltpu.VMEM((4, 4, 3, CH, 256), BF16),
            pltpu.VMEM((4, 3, CH, 256), F32),
            pltpu.VMEM((2, 2, 4, 4, 256, 256), BF16),
            pltpu.VMEM((2, 2, 2, 2, E, 128), BF16),
            pltpu.VMEM((2, 256, 256), BF16),
            pltpu.VMEM((2, 3, 256, E), BF16),
            pltpu.VMEM((256, 256), BF16),
            pltpu.VMEM((E, 256), BF16),
            pltpu.VMEM((2, 256, 256), BF16),
            pltpu.VMEM((1024, 256), BF16),
            pltpu.VMEM(field, F32),
            pltpu.VMEM(field, F32),
            pltpu.VMEM(field, F32),
            pltpu.VMEM((E + 6, E, 256), F32),
            pltpu.VMEM((E, E + 16, 256), F32),
            pltpu.VMEM((E, E, 256), F32),
            pltpu.VMEM((3, E, E, 256), F32),
            pltpu.VMEM((2, 1024, 128), F32),
            pltpu.VMEM((2, 1024, 128), F32),
            pltpu.VMEM((4, 2, 96, 256), BF16),
            pltpu.VMEM((3, 2, 96, 256), BF16),
            pltpu.VMEM((4, 2, E, 8, 256), F32),
            pltpu.VMEM((8, 256), jnp.int32),
            pltpu.VMEM((3, 8, 256), jnp.int32),
            pltpu.VMEM((3, 8, 256), jnp.int32),
            dma((4, 4, 8)),
            dma((4, 4, 8)),
            dma((4, 4)),
            dma((4, 4)),
            dma((6,)),
            dma((6,)),
            dma((5,)),
        ],
        compiler_params=pltpu.CompilerParams(
            collective_id=0, has_side_effects=True, vmem_limit_bytes=62 << 20
        ),
        name="gradient",
    )(
        index,
        template.reshape(1024, 256),
        target_image.reshape(1024, 256),
        velocity,
        operators.reshape(64, 96, E),
    )
    return vg, tg.reshape(E, E, 256)


def solution(mesh):
    placed = (
        P("gx", "gy", None),
        P("gx", "gy", None),
        P(None, "gx", "gy", None),
        P(),
        P(None, "gx", "gy", None, None),
        P(None, "gx", "gy", None),
        P(None, "gx", "gy", None),
    )
    return jax.shard_map(
        shards,
        mesh=mesh,
        in_specs=placed,
        out_specs=(P(None, "gx", "gy", None), P("gx", "gy", None)),
        check_vma=False,
    )
```

```python
import jax
import jax.numpy as jnp
from jax import lax
from jax.experimental import pallas as pl
from jax.experimental.pallas import tpu as pltpu
from jax.sharding import PartitionSpec as P

MESH = pl.DeviceIdType.MESH
F32 = jnp.float32
BF16 = jnp.bfloat16
E = 32
CH = 256
HF = 128


def mm(a, b):
    return jnp.dot(a, b, preferred_element_type=F32)


def mmt(a, b):
    return lax.dot_general(a, b, (((1,), (1,)), ((), ())), preferred_element_type=F32)


def iota(shape, dim):
    return lax.broadcasted_iota(jnp.int32, shape, dim)


def kernel(
    opi_ref, route_ref, brick_ref, tmpl_hbm, targ_hbm, vel_hbm, ops_hbm, vg_hbm, tg_ref,
    tmpl, ops_ref,
    f1, gg, r3, r12, ps, pf, sel, lhs, wc, ost, chosen, fold, mask, mask4, tile, dz, targ,
    qs0, qs1, qd, qv0, qv1, v2, out, s1f, l1f, hx, hxs, hy, meta, mz, my,
    xs, xr, hs, hs2, hr, ms, mr, ls,
):
    gx = lax.axis_index("gx")
    gy = lax.axis_index("gy")
    z = gx // 4
    y = gx % 4

    def at(dz_, dy_):
        return ((z + dz_) % 4) * 4 + (y + dy_) % 4

    ylo, yhi = (gy + 7) % 8, (gy + 1) % 8
    peers = [at(1, 0), at(3, 0), at(0, 1), at(0, 3)]

    barrier = pltpu.get_barrier_semaphore()
    for p in peers:
        pl.semaphore_signal(barrier, inc=1, device_id={"gx": p}, device_id_type=MESH)
    for p in (ylo, yhi):
        pl.semaphore_signal(barrier, inc=1, device_id={"gy": p}, device_id_type=MESH)

    tables = [
        pltpu.make_async_copy(ops_hbm, ops_ref, ls.at[5]),
        pltpu.make_async_copy(tmpl_hbm, tmpl, ls.at[6]),
    ]
    loads = [
        pltpu.make_async_copy(vel_hbm.at[0], qv0.at[pl.ds(3, E)], ls.at[0]),
        pltpu.make_async_copy(vel_hbm.at[1], qv1.at[:, pl.ds(8, E), :], ls.at[1]),
        pltpu.make_async_copy(vel_hbm.at[2], v2, ls.at[2]),
        pltpu.make_async_copy(targ_hbm, targ, ls.at[3]),
    ]
    for c in tables + loads:
        c.start()

    lane_b = iota((8, 256), 1) // E
    row_t = iota((8, 256), 0)
    m = jnp.zeros((8, 256), jnp.int32)
    for t in range(2):
        for b in range(8):
            m = jnp.where((row_t == t) & (lane_b == b), route_ref[t, 0, 0, b] * 8 + brick_ref[t, 0, 0, b], m)
    meta[...] = m

    mask[...] = jnp.where(iota((256, 256), 0) // E == iota((256, 256), 1) // E, 1.0, 0.0).astype(BF16)
    mask4[...] = jnp.concatenate([mask[0:128, 0:128]] * 2, axis=1)
    tile[...] = jnp.where(iota((E, 256), 0) == iota((E, 256), 1) % E, 1.0, 0.0).astype(BF16)

    fold[...] = jnp.where(iota((1024, E), 0) % E == iota((1024, E), 1), 1.0, 0.0).astype(BF16)
    entry = iota((16, 64), 1)
    row16 = iota((16, 64), 0)
    hot = jnp.zeros((16, 64), F32)
    for t in range(2):
        for b in range(8):
            hot = jnp.where((row16 == t * 8 + b) & (entry == opi_ref[t, 0, 0, b]), 1.0, hot)
    hot = hot.astype(BF16)
    tables[0].wait()
    for k in range(3):
        for n in range(4):
            chosen[k, :, n * 256:(n + 1) * 256] = mmt(hot, ops_ref[k * 1024 + n * 256:k * 1024 + (n + 1) * 256, :])

    def build(t):
        for k in range(3):
            keep = iota((E, 1024), 1) // E == iota((E, 1024), 0)
            rows = [
                jnp.where(keep, jnp.broadcast_to(chosen[k, t * 8 + b:t * 8 + b + 1, :], (E, 1024)), 0.0).astype(BF16)
                for b in range(8)
            ]
            ost[t, k] = mm(jnp.concatenate(rows, axis=0), fold[...]).astype(BF16)
        for k in range(2):
            for j in range(2):
                part = ost[t, k, j * 128:(j + 1) * 128, :]
                spread = mm(part, tile[:, 0:128]) * mask[0:128, 0:128].astype(F32)
                lhs[t, k, 0, j] = (spread[0:32] + spread[32:64] + spread[64:96] + spread[96:128]).astype(BF16)
                lhs[t, k, 1, j] = mmt(tile[:, 0:E], part).astype(BF16)
        wc[t] = (mm(ost[t, 2], tile[...]) * mask[...].astype(F32)).astype(BF16)

    build(0)

    sends = []

    def send(src, dst, ssem, rsem, dev):
        c = pltpu.make_async_remote_copy(
            src_ref=src, dst_ref=dst, send_sem=ssem, recv_sem=rsem, device_id=dev, device_id_type=MESH
        )
        return c

    def meta_copy(i):
        buf, half = ((mz, 0), (my, 3))[i // 3]
        n = i % 3
        d = (1, 3, 3)[n]
        src, dst = [(meta, buf.at[2]), (meta, buf.at[0]), (buf.at[0], buf.at[1])][n]
        dev = at(d, 0) if i < 3 else at(0, d)
        return send(src, dst, ms.at[i], mr.at[i], {"gx": dev})

    metas = [meta_copy(i) for i in range(6)]

    def halo_x(f, low, high):
        to_low, to_high = jnp.where(y == 0, 1, 0), jnp.where(y == 3, 1, 0)
        return [
            send(low, hx.at[f, 1, to_low], hs.at[f, 0], hr.at[f, 0, to_low], {"gx": at(0, 3)}),
            send(high, hx.at[f, 0, to_high], hs.at[f, 1], hr.at[f, 1, to_high], {"gx": at(0, 1)}),
        ]

    def relay(f, n):
        side = 1 - n
        return send(
            hx.at[f, side, 1], hx.at[f, side, 0], hs2.at[f, n], hr.at[f, n, 0], {"gx": at((3, 1)[n], 0)}
        )

    def hand_on(f):
        @pl.when(y == 3)
        def _():
            send(hx.at[f, 1, 1], hx.at[f, 1, 1], hs2.at[f, 0], hr.at[f, 0, 1], {"gx": at(0, 1)}).wait_recv()
            relay(f, 0).start()

        @pl.when(y == 0)
        def _():
            send(hx.at[f, 0, 1], hx.at[f, 0, 1], hs2.at[f, 1], hr.at[f, 1, 1], {"gx": at(0, 3)}).wait_recv()
            relay(f, 1).start()

    def wait_x(f):
        relay(f, 0).wait_recv()
        relay(f, 1).wait_recv()

    def halo_y(f, low, high):
        return [
            send(low, hy.at[f, 1], hs.at[f, 2], hr.at[f, 2, 0], {"gy": ylo}),
            send(high, hy.at[f, 0], hs.at[f, 3], hr.at[f, 3, 0], {"gy": yhi}),
        ]

    def contract(t, k, tr, load, store):
        for j in range(2):
            for i in range(0, 8, 2):
                part = jnp.concatenate([load(i, j), load(i + 1, j)], axis=1)
                big = jnp.concatenate([part] * 4, axis=0) * mask4[...]
                res = mm(lhs[t, k, tr, j], big)
                store(i, j, res[:, 0:128])
                store(i + 1, j, res[:, 128:256])

    def first(t, k, tr, row0, value):
        def load(i, j):
            return value[i * E:(i + 1) * E, j * 128:(j + 1) * 128]

        def store(i, j, res):
            f1[j, pl.ds(row0 + i * E, E), :] = res

        contract(t, k, tr, load, store)

    def second(t, k, tr, row0):
        got = [[None, None] for _ in range(8)]

        def load(i, j):
            return f1[j, pl.ds(row0 // E + i, E, stride=E), :].astype(BF16)

        def store(i, j, res):
            got[i][j] = res

        contract(t, k, tr, load, store)
        rows = [jnp.concatenate(g, axis=1) for g in got]
        return jnp.concatenate(rows, axis=0)

    def row_of(u):
        return pl.multiple_of((u % 2) * 512 + (u // 2) * CH, CH)

    def axes(p, u):
        a = (1 - u % 2) if p < 2 else u % 2
        gather = (at(a, 1 - a), at(3 * a, 3 * (1 - a)))
        scatter = (at(1 - a, a), at(3 * (1 - a), 3 * a))
        return gather, scatter

    def xcopy(p, u, n):
        (gp, gm), (sp, sm) = axes(p, u)
        own, up, far, down = [gg.at[p, u, :, pl.ds(n * 256, 256)] for n in range(4)]
        top, low = pl.ds(0, HF), pl.ds(HF, HF)
        src, dst, dev = [
            (own, down, gp),
            (own, up, gm),
            (down.at[top], far.at[top], gp),
            (up.at[low], far.at[low], gm),
            (ps.at[p, u, 0, top], r3.at[p, u, top], sp),
            (ps.at[p, u, 0, low], r3.at[p, u, low], sm),
            (ps.at[p, u, 1, top], r12.at[p, u, 0, top], sp),
            (ps.at[p, u, 2, low], r12.at[p, u, 1, low], sm),
            (ps.at[p, u, 1, low], r12.at[p, u, 0, low], sp),
            (ps.at[p, u, 2, top], r12.at[p, u, 1, top], sm),
        ][n]
        return send(src, dst, xs.at[p, u, n], xr.at[p, u, n], {"gx": dev})

    def units(body):
        def step(u, carry):
            body(u)
            return carry
        lax.fori_loop(0, 4, step, 0)

    def gather_start(p, u):
        xcopy(p, u, 0).start()
        xcopy(p, u, 1).start()

    def gather_on(p):
        def body(u):
            xcopy(p, u, 0).wait_recv()
            xcopy(p, u, 2).start()
            xcopy(p, u, 1).wait_recv()
            xcopy(p, u, 3).start()
        units(body)

    def pick(p, t):
        def body(u):
            xcopy(p, u, 2).wait_recv()
            xcopy(p, u, 3).wait_recv()
            h = u % 2
            held = [gg[p, u, :, n * 256:(n + 1) * 256] for n in range(4)]

            def part(o):
                total = None
                for s in range(4):
                    v = mmt(held[s], sel[t, h, o, s]) if p < 2 else mm(held[s], sel[t, h, s, o])
                    total = v if total is None else total + v
                return total

            ps[p, u, 0] = part(2).astype(BF16)
            xcopy(p, u, 4).start()
            xcopy(p, u, 5).start()
            v = part(1)
            pf[u, 0, 0:HF, :] = v[0:HF]
            ps[p, u, 1, HF:CH, :] = v[HF:CH].astype(BF16)
            v = part(3)
            pf[u, 0, HF:CH, :] = v[HF:CH]
            ps[p, u, 2, 0:HF, :] = v[0:HF].astype(BF16)
            pf[u, 1] = part(0)
        units(body)

    def scatter_on(p):
        def body(u):
            xcopy(p, u, 8).start()
            xcopy(p, u, 9).start()
            xcopy(p, u, 4).wait_recv()
            ps[p, u, 1, 0:HF, :] = (pf[u, 0, 0:HF, :] + r3[p, u, 0:HF, :].astype(F32)).astype(BF16)
            xcopy(p, u, 6).start()
            xcopy(p, u, 5).wait_recv()
            ps[p, u, 2, HF:CH, :] = (pf[u, 0, HF:CH, :] + r3[p, u, HF:CH, :].astype(F32)).astype(BF16)
            xcopy(p, u, 7).start()
        units(body)

    def arrived(p, u):
        for n in (8, 9, 6, 7):
            xcopy(p, u, n).wait_recv()
        return pf[u, 1] + r12[p, u, 0].astype(F32) + r12[p, u, 1].astype(F32)

    def build_sel(t):
        row = iota((256, 256), 0)
        same = row % E == iota((256, 256), 1) % E
        row_e = row // E
        for h in range(2):
            for s in range(4):
                raw = (meta if s == 0 else (mz, my)[h].at[s - 1])[t:t + 1, :]
                rz, ry, e = raw >> 5, (raw >> 3) & 3, raw & 7
                if h == 0:
                    key = jnp.where(rz == z, (((ry - y) & 3) << 3) | e, -1)
                else:
                    key = jnp.where(ry == y, (((rz - z) & 3) << 3) | e, -1)
                key = jnp.broadcast_to(key, (256, 256))
                for o in range(4):
                    sel[t, h, o, s] = jnp.where(same & (row_e + 8 * o == key), 1.0, 0.0).astype(BF16)

    xl = jnp.where(gx > 0, 1.0, 0.0).astype(F32)
    xh = jnp.where(gx < 15, 1.0, 0.0).astype(F32)
    yl = jnp.where(gy > 0, 1.0, 0.0).astype(F32)
    yh = jnp.where(gy < 7, 1.0, 0.0).astype(F32)

    def rim_x(f, q, off):
        for i in range(3):
            q[i, off:off + E, :] = hx[f, 0, 0, i * E:(i + 1) * E, :].astype(F32) * xl
            q[E + 3 + i, off:off + E, :] = hx[f, 1, 0, i * E:(i + 1) * E, :].astype(F32) * xh

    def rim_y(f, q, off):
        def step(i, c):
            q[off + i, 0:8, :] = hy[f, 0, i] * yl
            q[off + i, 40:48, :] = hy[f, 1, i] * yh
            return c
        lax.fori_loop(0, E, step, 0)

    def combine(p1, m1, p2, m2, p3, m3):
        return 0.75 * (p1 - m1) - 0.15 * (p2 - m2) + (p3 - m3) * (1.0 / 60.0)

    def d_x(q, i, off):
        at_ = [q[i + n, off:off + E, :] for n in range(7)]
        return combine(at_[4], at_[2], at_[5], at_[1], at_[6], at_[0])

    def d_y(q, i):
        at_ = [q[i, 5 + n:5 + n + E, :] for n in range(7)]
        return combine(at_[4], at_[2], at_[5], at_[1], at_[6], at_[0])

    diff = iota((256, 256), 0) - iota((256, 256), 1)
    size = jnp.abs(diff)
    coef = jnp.where(size == 1, 0.75, 0.0) + jnp.where(size == 2, -0.15, 0.0) + jnp.where(size == 3, 1.0 / 60.0, 0.0)
    coef = jnp.where(diff < 0, -coef, coef).astype(F32)
    dz_hi = coef.astype(BF16)
    dz[0] = dz_hi
    dz[1] = (coef - dz_hi.astype(F32)).astype(BF16)

    def d_z(value, exact):
        hi = value.astype(BF16)
        total = mm(hi, dz[0]) + mm(hi, dz[1])
        if not exact:
            total = total + mm((value - hi.astype(F32)).astype(BF16), dz[0])
        return total

    def planes(lo, hi, body):
        def step(i, c):
            body(i)
            return c
        lax.fori_loop(lo, hi, step, 0)

    def gradient(q, weight, lo, hi, exact):
        def group(g):
            i0 = g * 8
            dzv = d_z(q[pl.ds(3 + i0, 8), 8:8 + E, :].reshape(8 * E, 256), exact)
            for n in range(8):
                i = i0 + n
                w = weight(i)
                part = dzv[n * E:(n + 1) * E]
                if w is None:
                    out[0, i] = -0.25 * d_x(q, i + 0, 8)
                    out[1, i] = -0.25 * d_y(q, i + 3)
                    out[2, i] = -0.25 * part
                else:
                    out[0, i] = out[0, i] + w * d_x(q, i, 8)
                    out[1, i] = out[1, i] + w * d_y(q, i + 3)
                    out[2, i] = out[2, i] + w * part
        planes(lo, hi, group)

    tables[1].wait()

    def chunk0(u):
        r = pl.multiple_of(u * CH, CH)
        first(0, 1, 0, r, tmpl[pl.ds(r, CH), :])
    units(chunk0)

    def fill0(i):
        qs0[3 + i, 8:8 + E, :] = tmpl[pl.ds(pl.multiple_of(i * E, E), E), :].astype(F32)
    planes(0, E, fill0)

    pl.semaphore_wait(barrier, 6)

    for i in (0, 1, 3, 4):
        metas[i].start()

    def forward_start(p, t, k):
        def body(u):
            r = row_of(u)
            gg[p, u, :, 0:256] = mmt(second(t, k, 0, r).astype(BF16), wc[t]).astype(BF16)
            gather_start(p, u)
        units(body)

    forward_start(0, 0, 0)

    for c in loads:
        c.wait()
    for i in range(3):
        hxs[0, 0, i * E:(i + 1) * E, :] = qv0[3 + i].astype(BF16)
        hxs[0, 1, i * E:(i + 1) * E, :] = qv0[E + i].astype(BF16)
    velx = halo_x(1, hxs.at[0, 0], hxs.at[0, 1])
    vels = halo_y(1, qv1.at[:, pl.ds(8, 8), :], qv1.at[:, pl.ds(32, 8), :])
    tempx = halo_x(0, tmpl.at[pl.ds(0, 96)], tmpl.at[pl.ds(928, 96)])
    temps = halo_y(0, qs0.at[pl.ds(3, E), pl.ds(8, 8), :], qs0.at[pl.ds(3, E), pl.ds(32, 8), :])
    for c in velx + vels + tempx + temps:
        c.start()
    sends += velx + vels + tempx + temps
    for i in (1, 4):
        metas[i].wait_recv()
        metas[i + 1].start()
    for i in (0, 3, 2, 5):
        metas[i].wait_recv()
    build_sel(0)
    gather_on(0)
    hand_on(1)
    hand_on(0)
    build(1)
    pick(0, 0)
    scatter_on(0)

    for c in vels:
        c.wait_recv()
    wait_x(1)
    rim_x(1, qv0, 0)
    rim_y(1, qv1, 0)

    def div_group(g):
        i0 = g * 8
        dzv = d_z(v2[pl.ds(i0, 8)].reshape(8 * E, 256), False)
        for n in range(8):
            i = i0 + n
            qd[3 + i, 8:8 + E, :] = d_x(qv0, i, 0) + d_y(qv1, i) + dzv[n * E:(n + 1) * E]
    planes(0, 4, div_group)
    for i in range(3):
        hxs[1, 0, i * E:(i + 1) * E, :] = qd[3 + i, 8:8 + E, :].astype(BF16)
        hxs[1, 1, i * E:(i + 1) * E, :] = qd[E + i, 8:8 + E, :].astype(BF16)
    divx = halo_x(2, hxs.at[1, 0], hxs.at[1, 1])
    divs = halo_y(2, qd.at[pl.ds(3, E), pl.ds(8, 8), :], qd.at[pl.ds(3, E), pl.ds(32, 8), :])
    for c in divx + divs:
        c.start()
    sends += divx + divs
    build_sel(1)

    def end0(u):
        r = row_of(u)
        s1 = arrived(0, u).astype(BF16)
        wide = s1.astype(F32)
        s1f[0, pl.ds(r, CH), :] = wide[:, 0:128]
        s1f[1, pl.ds(r, CH), :] = wide[:, 128:256]
        first(1, 0, 0, r, s1)
    units(end0)

    forward_start(1, 1, 1)

    def fill1(i):
        qs1[3 + i, 8:8 + E, 0:128] = s1f[0, pl.ds(i, E, stride=E), :]
        qs1[3 + i, 8:8 + E, 128:256] = s1f[1, pl.ds(i, E, stride=E), :]
    planes(0, E, fill1)
    for i in range(3):
        hxs[2, 0, i * E:(i + 1) * E, :] = qs1[3 + i, 8:8 + E, :].astype(BF16)
        hxs[2, 1, i * E:(i + 1) * E, :] = qs1[E + i, 8:8 + E, :].astype(BF16)
    onex = halo_x(3, hxs.at[2, 0], hxs.at[2, 1])
    ones = halo_y(3, qs1.at[pl.ds(3, E), pl.ds(8, 8), :], qs1.at[pl.ds(3, E), pl.ds(32, 8), :])
    for c in onex + ones:
        c.start()
    sends += onex + ones
    gather_on(1)
    hand_on(2)
    pick(1, 1)
    hand_on(3)
    scatter_on(1)
    for c in divs:
        c.wait_recv()
    wait_x(2)
    rim_x(2, qd, 8)
    rim_y(2, qd, 3)
    gradient(qd, lambda i: None, 0, 4, False)

    def end1(u):
        r = row_of(u)
        s2 = arrived(1, u).astype(BF16).astype(F32)
        gg[2, u, :, 0:256] = (s2 - targ[pl.ds(r, CH), :].astype(F32)).astype(BF16)
        gather_start(2, u)
    units(end1)

    for c in ones:
        c.wait_recv()
    wait_x(3)
    rim_x(3, qs1, 8)
    rim_y(3, qs1, 3)

    def weight1(i):
        u = (i % 16) // 8 * 2 + i // 16
        return 0.5 * gg[2, u, pl.ds(pl.multiple_of(i % 8 * E, E), E), 0:256].astype(F32)
    gradient(qs1, weight1, 0, 2, True)
    gather_on(2)
    pick(2, 1)
    scatter_on(2)
    gradient(qs1, weight1, 2, 4, True)

    def end2(u):
        r = row_of(u)
        back = arrived(2, u).astype(BF16)
        first(1, 1, 1, r, mm(back, wc[1]).astype(BF16))
    units(end2)

    def adjoint_start(u):
        r = row_of(u)
        l1 = second(1, 0, 1, r).astype(BF16)
        gg[3, u, :, 0:256] = l1
        gather_start(3, u)
        wide = l1.astype(F32) * 0.5
        l1f[0, pl.ds(r, CH), :] = wide[:, 0:128]
        l1f[1, pl.ds(r, CH), :] = wide[:, 128:256]
    units(adjoint_start)

    for c in temps:
        c.wait_recv()
    wait_x(0)
    rim_x(0, qs0, 8)
    rim_y(0, qs0, 3)

    def weight0(i):
        return jnp.concatenate(
            [l1f[0, pl.ds(i, E, stride=E), :], l1f[1, pl.ds(i, E, stride=E), :]], axis=1
        )
    gradient(qs0, weight0, 0, 2, True)
    gather_on(3)
    pick(3, 0)
    scatter_on(3)
    gradient(qs0, weight0, 2, 4, True)
    save = pltpu.make_async_copy(out, vg_hbm, ls.at[4])
    save.start()

    def end3(u):
        r = row_of(u)
        back = arrived(3, u).astype(BF16)
        first(0, 0, 1, r, mm(back, wc[0]).astype(BF16))
    units(end3)

    def finish(u):
        r = row_of(u)
        tg_ref[pl.ds(r, CH), :] = second(0, 1, 1, r).astype(BF16)
    units(finish)

    for c in metas + sends:
        c.wait_send()

    @pl.when(y == 3)
    def _():
        for f in range(4):
            relay(f, 0).wait_send()

    @pl.when(y == 0)
    def _():
        for f in range(4):
            relay(f, 1).wait_send()

    for p in range(4):
        def drain(u, p=p):
            for n in range(10):
                xcopy(p, u, n).wait_send()
        units(drain)
    save.wait()


def shards(template, target_image, velocity, operators, route, target_brick, operator_index):
    vmem = pl.BlockSpec(memory_space=pltpu.VMEM)
    hbm = pl.BlockSpec(memory_space=pl.ANY)
    smem = pl.BlockSpec(memory_space=pltpu.SMEM)
    field = (E + 6, E + 16, 256)
    dma = pltpu.SemaphoreType.DMA
    vg, tg = pl.pallas_call(
        kernel,
        out_shape=(
            jax.ShapeDtypeStruct((3, E, E, 256), F32),
            jax.ShapeDtypeStruct((1024, 256), BF16),
        ),
        in_specs=[smem, smem, smem, hbm, hbm, hbm, hbm],
        out_specs=(hbm, vmem),
        scratch_shapes=[
            pltpu.VMEM((1024, 256), BF16),
            pltpu.VMEM((3 * E * E, 64), BF16),
            pltpu.VMEM((2, 1024, 128), F32),
            pltpu.VMEM((4, 4, CH, 1024), BF16),
            pltpu.VMEM((4, 4, CH, 256), BF16),
            pltpu.VMEM((4, 4, 2, CH, 256), BF16),
            pltpu.VMEM((4, 4, 3, CH, 256), BF16),
            pltpu.VMEM((4, 2, CH, 256), F32),
            pltpu.VMEM((2, 2, 4, 4, 256, 256), BF16),
            pltpu.VMEM((2, 2, 2, 2, E, 128), BF16),
            pltpu.VMEM((2, 256, 256), BF16),
            pltpu.VMEM((2, 3, 256, E), BF16),
            pltpu.VMEM((3, 16, 1024), F32),
            pltpu.VMEM((1024, E), BF16),
            pltpu.VMEM((256, 256), BF16),
            pltpu.VMEM((128, 256), BF16),
            pltpu.VMEM((E, 256), BF16),
            pltpu.VMEM((2, 256, 256), BF16),
            pltpu.VMEM((1024, 256), BF16),
            pltpu.VMEM(field, F32),
            pltpu.VMEM(field, F32),
            pltpu.VMEM(field, F32),
            pltpu.VMEM((E + 6, E, 256), F32),
            pltpu.VMEM((E, E + 16, 256), F32),
            pltpu.VMEM((E, E, 256), F32),
            pltpu.VMEM((3, E, E, 256), F32),
            pltpu.VMEM((2, 1024, 128), F32),
            pltpu.VMEM((2, 1024, 128), F32),
            pltpu.VMEM((4, 2, 2, 96, 256), BF16),
            pltpu.VMEM((3, 2, 96, 256), BF16),
            pltpu.VMEM((4, 2, E, 8, 256), F32),
            pltpu.VMEM((8, 256), jnp.int32),
            pltpu.VMEM((3, 8, 256), jnp.int32),
            pltpu.VMEM((3, 8, 256), jnp.int32),
            dma((4, 4, 10)),
            dma((4, 4, 10)),
            dma((4, 4)),
            dma((4, 2)),
            dma((4, 4, 2)),
            dma((6,)),
            dma((6,)),
            dma((7,)),
        ],
        compiler_params=pltpu.CompilerParams(
            collective_id=0, has_side_effects=True, vmem_limit_bytes=62 << 20
        ),
        name="gradient",
    )(
        operator_index,
        route.reshape(route.shape[:4]),
        target_brick,
        template.reshape(1024, 256),
        target_image.reshape(1024, 256),
        velocity,
        operators.transpose(1, 2, 3, 0).reshape(3 * E * E, -1),
    )
    return vg, tg.reshape(E, E, 256)


def solution(mesh):
    placed = (
        P("gx", "gy", None),
        P("gx", "gy", None),
        P(None, "gx", "gy", None),
        P(),
        P(None, "gx", "gy", None, None),
        P(None, "gx", "gy", None),
        P(None, "gx", "gy", None),
    )
    return jax.shard_map(
        shards,
        mesh=mesh,
        in_specs=placed,
        out_specs=(P(None, "gx", "gy", None), P("gx", "gy", None)),
        check_vma=False,
    )
```

```python
import jax
import jax.numpy as jnp
from jax import lax
from jax.experimental import pallas as pl
from jax.experimental.pallas import tpu as pltpu
from jax.sharding import PartitionSpec as P

MESH = pl.DeviceIdType.MESH
F32 = jnp.float32
BF16 = jnp.bfloat16
E = 32
CH = 256
HF = 128


def mm(a, b):
    return jnp.dot(a, b, preferred_element_type=F32)


def mmt(a, b):
    return lax.dot_general(a, b, (((1,), (1,)), ((), ())), preferred_element_type=F32)


def iota(shape, dim):
    return lax.broadcasted_iota(jnp.int32, shape, dim)


def kernel(
    opi_ref, route_ref, brick_ref, tmpl_hbm, targ_hbm, vel_hbm, ops_hbm, vg_hbm, half_ref, last_ref,
    tmpl, ops_ref,
    f1, gg, r3, r12, ps, pf, sel, lhs, wc, ost, chosen, fold, mask, mask4, tile, dz, targ,
    qs0, qs1, qd, qv0, qv1, v2, out, s1f, l1f, hx, hxs, hy, meta, mz, my,
    xs, xr, hs, hs2, hr, ms, mr, ls,
):
    gx = lax.axis_index("gx")
    gy = lax.axis_index("gy")
    z = gx // 4
    y = gx % 4

    def at(dz_, dy_):
        return ((z + dz_) % 4) * 4 + (y + dy_) % 4

    ylo, yhi = (gy + 7) % 8, (gy + 1) % 8
    peers = [at(1, 0), at(3, 0), at(0, 1), at(0, 3)]

    barrier = pltpu.get_barrier_semaphore()
    for p in peers:
        pl.semaphore_signal(barrier, inc=1, device_id={"gx": p}, device_id_type=MESH)
    for p in (ylo, yhi):
        pl.semaphore_signal(barrier, inc=1, device_id={"gy": p}, device_id_type=MESH)

    tables = [
        pltpu.make_async_copy(ops_hbm, ops_ref, ls.at[5]),
        pltpu.make_async_copy(tmpl_hbm, tmpl, ls.at[6]),
    ]
    loads = [
        pltpu.make_async_copy(vel_hbm.at[0], qv0.at[pl.ds(3, E)], ls.at[0]),
        pltpu.make_async_copy(vel_hbm.at[1], qv1.at[:, pl.ds(8, E), :], ls.at[1]),
        pltpu.make_async_copy(vel_hbm.at[2], v2, ls.at[2]),
        pltpu.make_async_copy(targ_hbm, targ, ls.at[3]),
    ]
    for c in tables + loads:
        c.start()

    lane_b = iota((8, 256), 1) // E
    row_t = iota((8, 256), 0)
    m = jnp.zeros((8, 256), jnp.int32)
    for t in range(2):
        for b in range(8):
            m = jnp.where((row_t == t) & (lane_b == b), route_ref[t, 0, 0, b] * 8 + brick_ref[t, 0, 0, b], m)
    meta[...] = m

    mask[...] = jnp.where(iota((256, 256), 0) // E == iota((256, 256), 1) // E, 1.0, 0.0).astype(BF16)
    mask4[...] = jnp.concatenate([mask[0:128, 0:128]] * 2, axis=1)
    tile[...] = jnp.where(iota((E, 256), 0) == iota((E, 256), 1) % E, 1.0, 0.0).astype(BF16)

    fold[...] = jnp.where(iota((1024, E), 0) % E == iota((1024, E), 1), 1.0, 0.0).astype(BF16)
    entry = iota((16, 64), 1)
    row16 = iota((16, 64), 0)
    hot = jnp.zeros((16, 64), F32)
    for t in range(2):
        for b in range(8):
            hot = jnp.where((row16 == t * 8 + b) & (entry == opi_ref[t, 0, 0, b]), 1.0, hot)
    hot = hot.astype(BF16)
    tables[0].wait()
    for k in range(3):
        for n in range(4):
            chosen[k, :, n * 256:(n + 1) * 256] = mmt(hot, ops_ref[k * 1024 + n * 256:k * 1024 + (n + 1) * 256, :])

    def build(t):
        for k in range(3):
            keep = iota((E, 1024), 1) // E == iota((E, 1024), 0)
            rows = [
                jnp.where(keep, jnp.broadcast_to(chosen[k, t * 8 + b:t * 8 + b + 1, :], (E, 1024)), 0.0).astype(BF16)
                for b in range(8)
            ]
            ost[t, k] = mm(jnp.concatenate(rows, axis=0), fold[...]).astype(BF16)
        for k in range(2):
            for j in range(2):
                part = ost[t, k, j * 128:(j + 1) * 128, :]
                spread = mm(part, tile[:, 0:128]) * mask[0:128, 0:128].astype(F32)
                lhs[t, k, 0, j] = (spread[0:32] + spread[32:64] + spread[64:96] + spread[96:128]).astype(BF16)
                lhs[t, k, 1, j] = mmt(tile[:, 0:E], part).astype(BF16)
        wc[t] = (mm(ost[t, 2], tile[...]) * mask[...].astype(F32)).astype(BF16)

    build(0)

    sends = []

    def send(src, dst, ssem, rsem, dev):
        c = pltpu.make_async_remote_copy(
            src_ref=src, dst_ref=dst, send_sem=ssem, recv_sem=rsem, device_id=dev, device_id_type=MESH
        )
        return c

    def meta_copy(i):
        buf, half = ((mz, 0), (my, 3))[i // 3]
        n = i % 3
        d = (1, 3, 3)[n]
        src, dst = [(meta, buf.at[2]), (meta, buf.at[0]), (buf.at[0], buf.at[1])][n]
        dev = at(d, 0) if i < 3 else at(0, d)
        return send(src, dst, ms.at[i], mr.at[i], {"gx": dev})

    metas = [meta_copy(i) for i in range(6)]

    def halo_x(f, low, high):
        to_low, to_high = jnp.where(y == 0, 1, 0), jnp.where(y == 3, 1, 0)
        return [
            send(low, hx.at[f, 1, to_low], hs.at[f, 0], hr.at[f, 0, to_low], {"gx": at(0, 3)}),
            send(high, hx.at[f, 0, to_high], hs.at[f, 1], hr.at[f, 1, to_high], {"gx": at(0, 1)}),
        ]

    def relay(f, n):
        side = 1 - n
        return send(
            hx.at[f, side, 1], hx.at[f, side, 0], hs2.at[f, n], hr.at[f, n, 0], {"gx": at((3, 1)[n], 0)}
        )

    def hand_on(f):
        @pl.when(y == 3)
        def _():
            send(hx.at[f, 1, 1], hx.at[f, 1, 1], hs2.at[f, 0], hr.at[f, 0, 1], {"gx": at(0, 1)}).wait_recv()
            relay(f, 0).start()

        @pl.when(y == 0)
        def _():
            send(hx.at[f, 0, 1], hx.at[f, 0, 1], hs2.at[f, 1], hr.at[f, 1, 1], {"gx": at(0, 3)}).wait_recv()
            relay(f, 1).start()

    def wait_x(f):
        relay(f, 0).wait_recv()
        relay(f, 1).wait_recv()

    def halo_y(f, low, high):
        return [
            send(low, hy.at[f, 1], hs.at[f, 2], hr.at[f, 2, 0], {"gy": ylo}),
            send(high, hy.at[f, 0], hs.at[f, 3], hr.at[f, 3, 0], {"gy": yhi}),
        ]

    def contract(t, k, tr, load, store):
        for j in range(2):
            for i in range(0, 8, 2):
                part = jnp.concatenate([load(i, j), load(i + 1, j)], axis=1)
                big = jnp.concatenate([part] * 4, axis=0) * mask4[...]
                res = mm(lhs[t, k, tr, j], big)
                store(i, j, res[:, 0:128])
                store(i + 1, j, res[:, 128:256])

    def first(t, k, tr, row0, value, into=None):
        into = f1 if into is None else into

        def load(i, j):
            return value[i * E:(i + 1) * E, j * 128:(j + 1) * 128]

        def store(i, j, res):
            into[j, pl.ds(row0 + i * E, E), :] = res.astype(into.dtype)

        contract(t, k, tr, load, store)

    def second(t, k, tr, row0):
        got = [[None, None] for _ in range(8)]

        def load(i, j):
            return f1[j, pl.ds(row0 // E + i, E, stride=E), :].astype(BF16)

        def store(i, j, res):
            got[i][j] = res

        contract(t, k, tr, load, store)
        rows = [jnp.concatenate(g, axis=1) for g in got]
        return jnp.concatenate(rows, axis=0)

    def row_of(u):
        return pl.multiple_of((u % 2) * 512 + (u // 2) * CH, CH)

    def axes(p, u):
        a = (1 - u % 2) if p < 2 else u % 2
        gather = (at(a, 1 - a), at(3 * a, 3 * (1 - a)))
        scatter = (at(1 - a, a), at(3 * (1 - a), 3 * a))
        return gather, scatter

    def xcopy(p, u, n):
        (gp, gm), (sp, sm) = axes(p, u)
        own, up, far, down = [gg.at[p, u, :, pl.ds(n * 256, 256)] for n in range(4)]
        top, low = pl.ds(0, HF), pl.ds(HF, HF)
        src, dst, dev = [
            (own, down, gp),
            (own, up, gm),
            (down.at[top], far.at[top], gp),
            (up.at[low], far.at[low], gm),
            (ps.at[p, u, 0, top], r3.at[p, u, top], sp),
            (ps.at[p, u, 0, low], r3.at[p, u, low], sm),
            (ps.at[p, u, 1, top], r12.at[p, u, 0, top], sp),
            (ps.at[p, u, 2, low], r12.at[p, u, 1, low], sm),
            (ps.at[p, u, 1, low], r12.at[p, u, 0, low], sp),
            (ps.at[p, u, 2, top], r12.at[p, u, 1, top], sm),
        ][n]
        return send(src, dst, xs.at[p, u, n], xr.at[p, u, n], {"gx": dev})

    def units(body):
        def step(u, carry):
            body(u)
            return carry
        lax.fori_loop(0, 4, step, 0)

    def gather_start(p, u):
        xcopy(p, u, 0).start()
        xcopy(p, u, 1).start()

    def gather_on(p):
        def body(u):
            xcopy(p, u, 0).wait_recv()
            xcopy(p, u, 2).start()
            xcopy(p, u, 1).wait_recv()
            xcopy(p, u, 3).start()
        units(body)

    def pick(p, t):
        def body(u):
            xcopy(p, u, 2).wait_recv()
            xcopy(p, u, 3).wait_recv()
            h = u % 2
            held = [gg[p, u, :, n * 256:(n + 1) * 256] for n in range(4)]

            def part(o):
                total = None
                for s in range(4):
                    v = mmt(held[s], sel[t, h, o, s]) if p < 2 else mm(held[s], sel[t, h, s, o])
                    total = v if total is None else total + v
                return total

            ps[p, u, 0] = part(2).astype(BF16)
            xcopy(p, u, 4).start()
            xcopy(p, u, 5).start()
            v = part(1)
            pf[u, 0, 0:HF, :] = v[0:HF]
            ps[p, u, 1, HF:CH, :] = v[HF:CH].astype(BF16)
            v = part(3)
            pf[u, 0, HF:CH, :] = v[HF:CH]
            ps[p, u, 2, 0:HF, :] = v[0:HF].astype(BF16)
            pf[u, 1] = part(0)
        units(body)

    def scatter_on(p):
        def body(u):
            xcopy(p, u, 8).start()
            xcopy(p, u, 9).start()
            xcopy(p, u, 4).wait_recv()
            ps[p, u, 1, 0:HF, :] = (pf[u, 0, 0:HF, :] + r3[p, u, 0:HF, :].astype(F32)).astype(BF16)
            xcopy(p, u, 6).start()
            xcopy(p, u, 5).wait_recv()
            ps[p, u, 2, HF:CH, :] = (pf[u, 0, HF:CH, :] + r3[p, u, HF:CH, :].astype(F32)).astype(BF16)
            xcopy(p, u, 7).start()
        units(body)

    def arrived(p, u):
        for n in (8, 9, 6, 7):
            xcopy(p, u, n).wait_recv()
        return pf[u, 1] + r12[p, u, 0].astype(F32) + r12[p, u, 1].astype(F32)

    def build_sel(t):
        row = iota((256, 256), 0)
        same = row % E == iota((256, 256), 1) % E
        row_e = row // E
        for h in range(2):
            for s in range(4):
                raw = (meta if s == 0 else (mz, my)[h].at[s - 1])[t:t + 1, :]
                rz, ry, e = raw >> 5, (raw >> 3) & 3, raw & 7
                if h == 0:
                    key = jnp.where(rz == z, (((ry - y) & 3) << 3) | e, -1)
                else:
                    key = jnp.where(ry == y, (((rz - z) & 3) << 3) | e, -1)
                key = jnp.broadcast_to(key, (256, 256))
                for o in range(4):
                    sel[t, h, o, s] = jnp.where(same & (row_e + 8 * o == key), 1.0, 0.0).astype(BF16)

    xl = jnp.where(gx > 0, 1.0, 0.0).astype(F32)
    xh = jnp.where(gx < 15, 1.0, 0.0).astype(F32)
    yl = jnp.where(gy > 0, 1.0, 0.0).astype(F32)
    yh = jnp.where(gy < 7, 1.0, 0.0).astype(F32)

    def rim_x(f, q, off):
        for i in range(3):
            q[i, off:off + E, :] = hx[f, 0, 0, i * E:(i + 1) * E, :].astype(F32) * xl
            q[E + 3 + i, off:off + E, :] = hx[f, 1, 0, i * E:(i + 1) * E, :].astype(F32) * xh

    def rim_y(f, q, off):
        def step(i, c):
            q[off + i, 0:8, :] = hy[f, 0, i] * yl
            q[off + i, 40:48, :] = hy[f, 1, i] * yh
            return c
        lax.fori_loop(0, E, step, 0)

    def combine(p1, m1, p2, m2, p3, m3):
        return 0.75 * (p1 - m1) - 0.15 * (p2 - m2) + (p3 - m3) * (1.0 / 60.0)

    def d_x(q, i, off):
        at_ = [q[i + n, off:off + E, :] for n in range(7)]
        return combine(at_[4], at_[2], at_[5], at_[1], at_[6], at_[0])

    def d_y(q, i):
        at_ = [q[i, 5 + n:5 + n + E, :] for n in range(7)]
        return combine(at_[4], at_[2], at_[5], at_[1], at_[6], at_[0])

    diff = iota((256, 256), 0) - iota((256, 256), 1)
    size = jnp.abs(diff)
    coef = jnp.where(size == 1, 0.75, 0.0) + jnp.where(size == 2, -0.15, 0.0) + jnp.where(size == 3, 1.0 / 60.0, 0.0)
    coef = jnp.where(diff < 0, -coef, coef).astype(F32)
    dz_hi = coef.astype(BF16)
    dz[0] = dz_hi
    dz[1] = (coef - dz_hi.astype(F32)).astype(BF16)

    def d_z(value, exact):
        hi = value.astype(BF16)
        total = mm(hi, dz[0]) + mm(hi, dz[1])
        if not exact:
            total = total + mm((value - hi.astype(F32)).astype(BF16), dz[0])
        return total

    def planes(lo, hi, body):
        def step(i, c):
            body(i)
            return c
        lax.fori_loop(lo, hi, step, 0)

    def gradient(q, weight, lo, hi, exact):
        def group(g):
            i0 = g * 8
            dzv = d_z(q[pl.ds(3 + i0, 8), 8:8 + E, :].reshape(8 * E, 256), exact)
            for n in range(8):
                i = i0 + n
                w = weight(i)
                part = dzv[n * E:(n + 1) * E]
                if w is None:
                    out[0, i] = -0.25 * d_x(q, i + 0, 8)
                    out[1, i] = -0.25 * d_y(q, i + 3)
                    out[2, i] = -0.25 * part
                else:
                    out[0, i] = out[0, i] + w * d_x(q, i, 8)
                    out[1, i] = out[1, i] + w * d_y(q, i + 3)
                    out[2, i] = out[2, i] + w * part
        planes(lo, hi, group)

    tables[1].wait()

    def chunk0(u):
        r = pl.multiple_of(u * CH, CH)
        first(0, 1, 0, r, tmpl[pl.ds(r, CH), :])
    units(chunk0)

    def fill0(i):
        qs0[3 + i, 8:8 + E, :] = tmpl[pl.ds(pl.multiple_of(i * E, E), E), :].astype(F32)
    planes(0, E, fill0)

    pl.semaphore_wait(barrier, 6)

    for i in (0, 1, 3, 4):
        metas[i].start()

    def forward_start(p, t, k):
        def body(u):
            r = row_of(u)
            gg[p, u, :, 0:256] = mmt(second(t, k, 0, r).astype(BF16), wc[t]).astype(BF16)
            gather_start(p, u)
        units(body)

    forward_start(0, 0, 0)

    for c in loads:
        c.wait()
    for i in range(3):
        hxs[0, 0, i * E:(i + 1) * E, :] = qv0[3 + i].astype(BF16)
        hxs[0, 1, i * E:(i + 1) * E, :] = qv0[E + i].astype(BF16)
    velx = halo_x(1, hxs.at[0, 0], hxs.at[0, 1])
    vels = halo_y(1, qv1.at[:, pl.ds(8, 8), :], qv1.at[:, pl.ds(32, 8), :])
    tempx = halo_x(0, tmpl.at[pl.ds(0, 96)], tmpl.at[pl.ds(928, 96)])
    temps = halo_y(0, qs0.at[pl.ds(3, E), pl.ds(8, 8), :], qs0.at[pl.ds(3, E), pl.ds(32, 8), :])
    for c in velx + vels + tempx + temps:
        c.start()
    sends += velx + vels + tempx + temps
    for i in (1, 4):
        metas[i].wait_recv()
        metas[i + 1].start()
    for i in (0, 3, 2, 5):
        metas[i].wait_recv()
    build_sel(0)
    gather_on(0)
    hand_on(1)
    hand_on(0)
    build(1)
    pick(0, 0)
    scatter_on(0)

    for c in vels:
        c.wait_recv()
    wait_x(1)
    rim_x(1, qv0, 0)
    rim_y(1, qv1, 0)

    def div_group(g):
        i0 = g * 8
        dzv = d_z(v2[pl.ds(i0, 8)].reshape(8 * E, 256), False)
        for n in range(8):
            i = i0 + n
            qd[3 + i, 8:8 + E, :] = d_x(qv0, i, 0) + d_y(qv1, i) + dzv[n * E:(n + 1) * E]
    planes(0, 4, div_group)
    for i in range(3):
        hxs[1, 0, i * E:(i + 1) * E, :] = qd[3 + i, 8:8 + E, :].astype(BF16)
        hxs[1, 1, i * E:(i + 1) * E, :] = qd[E + i, 8:8 + E, :].astype(BF16)
    divx = halo_x(2, hxs.at[1, 0], hxs.at[1, 1])
    divs = halo_y(2, qd.at[pl.ds(3, E), pl.ds(8, 8), :], qd.at[pl.ds(3, E), pl.ds(32, 8), :])
    for c in divx + divs:
        c.start()
    sends += divx + divs
    build_sel(1)

    def end0(u):
        r = row_of(u)
        s1 = arrived(0, u).astype(BF16)
        wide = s1.astype(F32)
        s1f[0, pl.ds(r, CH), :] = wide[:, 0:128]
        s1f[1, pl.ds(r, CH), :] = wide[:, 128:256]
        first(1, 0, 0, r, s1)
    units(end0)

    forward_start(1, 1, 1)

    def fill1(i):
        qs1[3 + i, 8:8 + E, 0:128] = s1f[0, pl.ds(i, E, stride=E), :]
        qs1[3 + i, 8:8 + E, 128:256] = s1f[1, pl.ds(i, E, stride=E), :]
    planes(0, E, fill1)
    for i in range(3):
        hxs[2, 0, i * E:(i + 1) * E, :] = qs1[3 + i, 8:8 + E, :].astype(BF16)
        hxs[2, 1, i * E:(i + 1) * E, :] = qs1[E + i, 8:8 + E, :].astype(BF16)
    onex = halo_x(3, hxs.at[2, 0], hxs.at[2, 1])
    ones = halo_y(3, qs1.at[pl.ds(3, E), pl.ds(8, 8), :], qs1.at[pl.ds(3, E), pl.ds(32, 8), :])
    for c in onex + ones:
        c.start()
    sends += onex + ones
    gather_on(1)
    hand_on(2)
    pick(1, 1)
    hand_on(3)
    scatter_on(1)
    for c in divs:
        c.wait_recv()
    wait_x(2)
    rim_x(2, qd, 8)
    rim_y(2, qd, 3)
    gradient(qd, lambda i: None, 0, 4, False)

    def end1(u):
        r = row_of(u)
        s2 = arrived(1, u).astype(BF16).astype(F32)
        gg[2, u, :, 0:256] = (s2 - targ[pl.ds(r, CH), :].astype(F32)).astype(BF16)
        gather_start(2, u)
    units(end1)

    for c in ones:
        c.wait_recv()
    wait_x(3)
    rim_x(3, qs1, 8)
    rim_y(3, qs1, 3)

    def weight1(i):
        u = (i % 16) // 8 * 2 + i // 16
        return 0.5 * gg[2, u, pl.ds(pl.multiple_of(i % 8 * E, E), E), 0:256].astype(F32)
    gradient(qs1, weight1, 0, 2, True)
    gather_on(2)
    pick(2, 1)
    scatter_on(2)
    gradient(qs1, weight1, 2, 4, True)

    def end2(u):
        r = row_of(u)
        back = arrived(2, u).astype(BF16)
        first(1, 1, 1, r, mm(back, wc[1]).astype(BF16))
    units(end2)

    def adjoint_start(u):
        r = row_of(u)
        l1 = second(1, 0, 1, r).astype(BF16)
        gg[3, u, :, 0:256] = l1
        gather_start(3, u)
        wide = l1.astype(F32) * 0.5
        l1f[0, pl.ds(r, CH), :] = wide[:, 0:128]
        l1f[1, pl.ds(r, CH), :] = wide[:, 128:256]
    units(adjoint_start)

    for c in temps:
        c.wait_recv()
    wait_x(0)
    rim_x(0, qs0, 8)
    rim_y(0, qs0, 3)

    def weight0(i):
        return jnp.concatenate(
            [l1f[0, pl.ds(i, E, stride=E), :], l1f[1, pl.ds(i, E, stride=E), :]], axis=1
        )
    gradient(qs0, weight0, 0, 2, True)
    gather_on(3)
    pick(3, 0)
    scatter_on(3)
    gradient(qs0, weight0, 2, 4, True)
    save = pltpu.make_async_copy(out, vg_hbm, ls.at[4])
    save.start()

    def end3(u):
        r = row_of(u)
        back = arrived(3, u).astype(BF16)
        first(0, 0, 1, r, mm(back, wc[0]).astype(BF16), half_ref)
    units(end3)

    for j in range(2):
        last_ref[j] = lhs[0, 1, 1, j]

    for c in metas + sends:
        c.wait_send()

    @pl.when(y == 3)
    def _():
        for f in range(4):
            relay(f, 0).wait_send()

    @pl.when(y == 0)
    def _():
        for f in range(4):
            relay(f, 1).wait_send()

    for p in range(4):
        def drain(u, p=p):
            for n in range(10):
                xcopy(p, u, n).wait_send()
        units(drain)
    save.wait()


def finish(half_hbm, last_ref, vg_in, vg_out, tg_ref, half, wide, mask, held, ls):
    load = pltpu.make_async_copy(half_hbm, half, ls.at[0])
    load.start()
    fetches = [pltpu.make_async_copy(vg_in.at[k], held.at[k], ls.at[1 + k]) for k in range(3)]
    copies = [pltpu.make_async_copy(held.at[k], vg_out.at[k], ls.at[4 + k]) for k in range(3)]
    for c in fetches:
        c.start()
    mask[...] = jnp.where(iota((128, 256), 0) // E == iota((128, 256), 1) % 128 // E, 1.0, 0.0).astype(BF16)
    load.wait()

    def widen(u, carry):
        r = pl.multiple_of(u * CH, CH)
        for j in range(2):
            wide[j, pl.ds(r, CH), :] = half[j, pl.ds(r, CH), :].astype(F32)
        return carry
    lax.fori_loop(0, 4, widen, 0)

    def body(u, carry):
        r = pl.multiple_of(u * CH, CH)
        for j in range(2):
            for i in range(0, 8, 2):
                pair = [wide[j, pl.ds(u * 8 + i + n, E, stride=E), :].astype(BF16) for n in range(2)]
                big = jnp.concatenate([jnp.concatenate(pair, axis=1)] * 4, axis=0) * mask[...]
                res = mm(last_ref[j], big).astype(BF16)
                for n in range(2):
                    tg_ref[pl.ds(r + (i + n) * E, E), j * 128:(j + 1) * 128] = res[:, n * 128:(n + 1) * 128]
        return carry
    lax.fori_loop(0, 2, body, 0)
    for k in range(3):
        fetches[k].wait()
        copies[k].start()
    lax.fori_loop(2, 4, body, 0)
    for c in copies:
        c.wait()


def shards(template, target_image, velocity, operators, route, target_brick, operator_index):
    vmem = pl.BlockSpec(memory_space=pltpu.VMEM)
    hbm = pl.BlockSpec(memory_space=pl.ANY)
    smem = pl.BlockSpec(memory_space=pltpu.SMEM)
    field = (E + 6, E + 16, 256)
    dma = pltpu.SemaphoreType.DMA
    part, half, last = pl.pallas_call(
        kernel,
        out_shape=(
            jax.ShapeDtypeStruct((3, E, E, 256), F32),
            jax.ShapeDtypeStruct((2, 1024, 128), BF16),
            jax.ShapeDtypeStruct((2, E, 128), BF16),
        ),
        in_specs=[smem, smem, smem, hbm, hbm, hbm, hbm],
        out_specs=(hbm, vmem, vmem),
        scratch_shapes=[
            pltpu.VMEM((1024, 256), BF16),
            pltpu.VMEM((3 * E * E, 64), BF16),
            pltpu.VMEM((2, 1024, 128), F32),
            pltpu.VMEM((4, 4, CH, 1024), BF16),
            pltpu.VMEM((4, 4, CH, 256), BF16),
            pltpu.VMEM((4, 4, 2, CH, 256), BF16),
            pltpu.VMEM((4, 4, 3, CH, 256), BF16),
            pltpu.VMEM((4, 2, CH, 256), F32),
            pltpu.VMEM((2, 2, 4, 4, 256, 256), BF16),
            pltpu.VMEM((2, 2, 2, 2, E, 128), BF16),
            pltpu.VMEM((2, 256, 256), BF16),
            pltpu.VMEM((2, 3, 256, E), BF16),
            pltpu.VMEM((3, 16, 1024), F32),
            pltpu.VMEM((1024, E), BF16),
            pltpu.VMEM((256, 256), BF16),
            pltpu.VMEM((128, 256), BF16),
            pltpu.VMEM((E, 256), BF16),
            pltpu.VMEM((2, 256, 256), BF16),
            pltpu.VMEM((1024, 256), BF16),
            pltpu.VMEM(field, F32),
            pltpu.VMEM(field, F32),
            pltpu.VMEM(field, F32),
            pltpu.VMEM((E + 6, E, 256), F32),
            pltpu.VMEM((E, E + 16, 256), F32),
            pltpu.VMEM((E, E, 256), F32),
            pltpu.VMEM((3, E, E, 256), F32),
            pltpu.VMEM((2, 1024, 128), F32),
            pltpu.VMEM((2, 1024, 128), F32),
            pltpu.VMEM((4, 2, 2, 96, 256), BF16),
            pltpu.VMEM((3, 2, 96, 256), BF16),
            pltpu.VMEM((4, 2, E, 8, 256), F32),
            pltpu.VMEM((8, 256), jnp.int32),
            pltpu.VMEM((3, 8, 256), jnp.int32),
            pltpu.VMEM((3, 8, 256), jnp.int32),
            dma((4, 4, 10)),
            dma((4, 4, 10)),
            dma((4, 4)),
            dma((4, 2)),
            dma((4, 4, 2)),
            dma((6,)),
            dma((6,)),
            dma((7,)),
        ],
        compiler_params=pltpu.CompilerParams(
            collective_id=0, has_side_effects=True, vmem_limit_bytes=62 << 20
        ),
        name="gradient",
    )(
        operator_index,
        route.reshape(route.shape[:4]),
        target_brick,
        template.reshape(1024, 256),
        target_image.reshape(1024, 256),
        velocity,
        operators.transpose(1, 2, 3, 0).reshape(3 * E * E, -1),
    )
    vg, tg = pl.pallas_call(
        finish,
        out_shape=(
            jax.ShapeDtypeStruct((3, E, E, 256), F32),
            jax.ShapeDtypeStruct((1024, 256), BF16),
        ),
        in_specs=[hbm, vmem, hbm],
        out_specs=(hbm, vmem),
        scratch_shapes=[
            pltpu.VMEM((2, 1024, 128), BF16),
            pltpu.VMEM((2, 1024, 128), F32),
            pltpu.VMEM((128, 256), BF16),
            pltpu.VMEM((3, E, E, 256), F32),
            dma((7,)),
        ],
        compiler_params=pltpu.CompilerParams(vmem_limit_bytes=62 << 20),
        name="finish",
    )(half, last, part)
    return vg, tg.reshape(E, E, 256)


def solution(mesh):
    placed = (
        P("gx", "gy", None),
        P("gx", "gy", None),
        P(None, "gx", "gy", None),
        P(),
        P(None, "gx", "gy", None, None),
        P(None, "gx", "gy", None),
        P(None, "gx", "gy", None),
    )
    return jax.shard_map(
        shards,
        mesh=mesh,
        in_specs=placed,
        out_specs=(P(None, "gx", "gy", None), P("gx", "gy", None)),
        check_vma=False,
    )
```
